512 devices in a mesh: seq: 64 (over y_lo, z, core), tp: 8 (over y_hi, x).
Axes of the slice: x: 4, y: 8 (y_hi: 2, y_lo: 4; y = y_hi * 4 + y_lo), z: 8, core: 2. Of those that a mesh axis runs over, the one named last changes fastest.
Arguments:
- queries: bfloat16 [8192, 16384], P('seq', 'tp'), may hold values from -64 to 64
- keys: bfloat16 [8192, 1024], P('seq', 'tp'), may hold values from -32 to 32
- values: bfloat16 [8192, 1024], P('seq', 'tp'), may hold values from -6 to 6
- block_start: int32 [64, 2], replicated, may hold values from 0 to 8128, as said below
Outputs:
- attended: bfloat16 [8192, 16384], P(('seq', 'tp'))
The draws below stay inside these ranges and needn't reach their ends.
Inputs may be any that keep to these rules, and one draw needn't show every extreme that they name: `block_start`: the entries are the multiples of 64 below 8192, each exactly once: the document's half-blocks in a drawn order.
All inputs are finite; a program needn't handle non-finite values.
Results may differ from the reference program's by a relative error of at most 0.008.
Values may be sent and summed in bfloat16 or wider, within the bound.
No kernel may reach another device: no remote copies, remote signals or barrier semaphores. Data moves between devices by JAX's collectives and lax.ppermute only.
A program may use at most 64 MiB of HBM per device.

```python
import math
import jax
import jax.numpy as jnp
from jax import lax

HEAD_SIZE = 128
QUERY_HEADS = 128
KEY_VALUE_HEADS = 8
TOK_DEV = 128
WINDOW_TOKENS = 8192


def draw_queries(key, part):
    key = jax.random.fold_in(key, 11)
    first_half = jax.random.fold_in(key, 0)
    base_offset = jax.random.truncated_normal(first_half, -6.0, 6.0, (WINDOW_TOKENS, QUERY_HEADS * HEAD_SIZE), jnp.float32)
    return base_offset.astype(jnp.bfloat16)


def draw_keys(key, part):
    key = jax.random.fold_in(key, 23)
    first_half = jax.random.fold_in(key, 0)
    base_offset = jax.random.truncated_normal(first_half, -6.0, 6.0, (WINDOW_TOKENS, KEY_VALUE_HEADS * HEAD_SIZE), jnp.float32)
    return base_offset.astype(jnp.bfloat16)


def draw_block_start(key, part):
    key = jax.random.fold_in(key, 37)
    half_rows = TOK_DEV // 2
    count = WINDOW_TOKENS // half_rows
    order = jax.random.permutation(key, count)
    return (order.reshape(count // 2, 2) * half_rows).astype(jnp.int32)


def levels(own_key, shape, cuts, least, high):
    level = 1.0
    for dim, shards_of in cuts:
        heights = jax.random.uniform(jax.random.fold_in(jax.random.fold_in(own_key, 6), dim), (shards_of,), jnp.float32, least / len(cuts), high / len(cuts))
        level = level * jnp.repeat(jnp.exp(heights), shape[dim] // shards_of).reshape((-1,) + (1,) * (len(shape) - 1 - dim))
    return level


def noise(rng, dims, spread, reach, cuts=(), held_as=jnp.bfloat16):
    loudness = levels(rng, dims, cuts, -0.22, 0.18) if cuts else 1.0
    drawn = jax.random.normal(rng, dims, jnp.float32) * spread * loudness
    return jnp.minimum(jnp.maximum(drawn, -reach), reach).astype(held_as)


def setup_inputs(seed: int = 0) -> dict:
    key_of = jax.random.split(jax.random.key(seed), 5)
    queries = draw_queries(jax.random.fold_in(key_of[4], 71), 0)
    keys = draw_keys(jax.random.fold_in(key_of[4], 71), 0)
    values = noise(key_of[2], (WINDOW_TOKENS, KEY_VALUE_HEADS * HEAD_SIZE), 1.0, 6.0, ((0, 64), (1, 8)))
    block_start = draw_block_start(jax.random.fold_in(key_of[4], 71), 0)
    return {"queries": queries, "keys": keys, "values": values, "block_start": block_start}


def reference(queries, keys, values, block_start):
    half_rows = TOK_DEV // 2
    row_ids = jnp.arange(WINDOW_TOKENS, dtype=jnp.int32)
    positions = block_start.reshape(-1)[row_ids // half_rows] + row_ids % half_rows
    heads_per_group = QUERY_HEADS // KEY_VALUE_HEADS
    block_size = math.gcd(512, WINDOW_TOKENS)
    block_count = WINDOW_TOKENS // block_size
    score_scale = HEAD_SIZE ** -0.5
    outputs = []
    for head_number in range(KEY_VALUE_HEADS):
        key_head = keys[:, head_number * HEAD_SIZE:(head_number + 1) * HEAD_SIZE].astype(jnp.float32)
        value_head = values[:, head_number * HEAD_SIZE:(head_number + 1) * HEAD_SIZE].astype(jnp.float32)
        query_head = queries[:, head_number * heads_per_group * HEAD_SIZE:(head_number + 1) * heads_per_group * HEAD_SIZE]
        query_head = query_head.reshape(WINDOW_TOKENS, heads_per_group, HEAD_SIZE).astype(jnp.float32)

        def one_block(block_index):
            begin = (block_index * block_size).astype(jnp.int32)
            query_block = lax.dynamic_slice_in_dim(query_head, begin, block_size, 0)
            query_pos = lax.dynamic_slice_in_dim(positions, begin, block_size, 0)
            scores = jnp.einsum("qjd,kd->qjk", query_block, key_head) * score_scale
            visible = (positions[None, :] <= query_pos[:, None])[:, None, :]
            scores = jnp.where(visible, scores, -jnp.inf)
            row_max = jnp.max(scores, axis=-1, keepdims=True)
            weights = jnp.where(visible, jnp.exp(scores - row_max), 0.0)
            denominator = jnp.sum(weights, axis=-1)
            rounded = lax.optimization_barrier(weights.astype(jnp.bfloat16)).astype(jnp.float32)
            weighted = jnp.einsum("qjk,kd->qjd", rounded, value_head)
            return (weighted / denominator[..., None]).reshape(block_size, heads_per_group * HEAD_SIZE)

        head_out = lax.map(one_block, jnp.arange(block_count, dtype=jnp.int32))
        outputs.append(head_out.reshape(WINDOW_TOKENS, heads_per_group * HEAD_SIZE))
    return jnp.concatenate(outputs, axis=1).astype(jnp.bfloat16)
```

```python
import math

import jax
import jax.numpy as jnp
from jax import lax
from jax.experimental import pallas as pl
from jax.experimental.pallas import tpu as pltpu
from jax.sharding import PartitionSpec as P

HEAD_SIZE = 128
HALF_ROWS = 64
MASKED_SCORE = -1e30
COLUMN_CHIPS = 4
PLANE_DEVICES = 16
ROW_TILE = 256
KEY_CHUNK = 1024


def attend_kernel(place_ref, own_ref, query_ref, kv_ref, out_ref, scaled, total, largest):
    heads = query_ref.shape[1] // HEAD_SIZE
    half_height = heads * HALF_ROWS
    chunk_blocks = KEY_CHUNK // HALF_ROWS
    scale = math.log2(math.e) / math.sqrt(HEAD_SIZE)
    for half in range(2):
        for head in range(heads):
            part = query_ref[
                half * HALF_ROWS : (half + 1) * HALF_ROWS,
                head * HEAD_SIZE : (head + 1) * HEAD_SIZE,
            ]
            part = part.astype(jnp.float32) * scale
            high = part.astype(jnp.bfloat16)
            start = half * half_height + head * HALF_ROWS
            scaled[start : start + HALF_ROWS, :HEAD_SIZE] = high
            scaled[start : start + HALF_ROWS, HEAD_SIZE:] = (
                part - high.astype(jnp.float32)
            ).astype(jnp.bfloat16)
    total[...] = jnp.zeros_like(total)
    largest[...] = jnp.full_like(largest, MASKED_SCORE)
    ones = jnp.ones((KEY_CHUNK, HEAD_SIZE), jnp.bfloat16)

    def absorb(chunk, halves, masked):
        rows_of = [
            kv_ref[
                pl.ds(
                    pl.multiple_of(place_ref[chunk * chunk_blocks + i] * HALF_ROWS, HALF_ROWS),
                    HALF_ROWS,
                ),
                :,
            ]
            for i in range(chunk_blocks)
        ]
        kv = jnp.concatenate(rows_of, axis=0)
        keys = kv[:, :HEAD_SIZE]
        keys = jnp.concatenate([keys, keys], axis=1)
        values = jnp.concatenate([kv[:, HEAD_SIZE:], ones], axis=1)
        for half in halves:
            for tile in range(half_height // ROW_TILE):
                start = half * half_height + tile * ROW_TILE
                rows = slice(start, start + ROW_TILE)
                scores = lax.dot_general(
                    scaled[rows, :],
                    keys,
                    (((1,), (1,)), ((), ())),
                    preferred_element_type=jnp.float32,
                )
                if masked:
                    shape = (ROW_TILE, KEY_CHUNK)
                    row_pos = own_ref[half] + lax.rem(
                        lax.broadcasted_iota(jnp.int32, shape, 0), HALF_ROWS
                    )
                    key_pos = chunk * KEY_CHUNK + lax.broadcasted_iota(jnp.int32, shape, 1)
                    scores = jnp.where(key_pos <= row_pos, scores, MASKED_SCORE)
                old = largest[rows, :]
                new = jnp.maximum(old, jnp.max(scores, axis=1, keepdims=True))
                weights = jnp.exp2(scores - new[:, :1]).astype(jnp.bfloat16)
                fade = jnp.exp2(old - new)
                product = jnp.dot(weights, values, preferred_element_type=jnp.float32)
                total[rows, :] = total[rows, :] * jnp.concatenate([fade, fade], axis=1) + product
                largest[rows, :] = new

    def absorb_run(first, end, halves):
        def body(chunk, carry):
            absorb(chunk, halves, False)
            return carry

        lax.fori_loop(first, end, body, 0)

    last = [own_ref[half] // KEY_CHUNK for half in range(2)]
    shared = jnp.minimum(last[0], last[1])
    absorb_run(0, shared, (0, 1))
    for half in range(2):
        absorb_run(shared, last[half], (half,))
        absorb(last[half], (half,), True)
    for half in range(2):
        for head in range(heads):
            start = half * half_height + head * HALF_ROWS
            rows = slice(start, start + HALF_ROWS)
            out_ref[
                half * HALF_ROWS : (half + 1) * HALF_ROWS,
                head * HEAD_SIZE : (head + 1) * HEAD_SIZE,
            ] = (total[rows, :HEAD_SIZE] / total[rows, HEAD_SIZE:]).astype(jnp.bfloat16)


def attend(queries, kv, place, own_starts):
    row_count = queries.shape[0] * queries.shape[1] // HEAD_SIZE
    return pl.pallas_call(
        attend_kernel,
        out_shape=jax.ShapeDtypeStruct(queries.shape, jnp.bfloat16),
        in_specs=[pl.BlockSpec(memory_space=pltpu.SMEM)] * 2
        + [pl.BlockSpec(memory_space=pltpu.VMEM)] * 2,
        out_specs=pl.BlockSpec(memory_space=pltpu.VMEM),
        scratch_shapes=[
            pltpu.VMEM((row_count, 2 * HEAD_SIZE), jnp.bfloat16),
            pltpu.VMEM((row_count, 2 * HEAD_SIZE), jnp.float32),
            pltpu.VMEM((row_count, HEAD_SIZE), jnp.float32),
        ],
        compiler_params=pltpu.CompilerParams(vmem_limit_bytes=56 * 2**20),
        name="attend",
    )(place, own_starts, queries, kv)


def on_device(queries, keys, values, block_start):
    own_index = lax.axis_index("seq")
    columns = [
        [chip * PLANE_DEVICES + place for chip in range(COLUMN_CHIPS)]
        for place in range(PLANE_DEVICES)
    ]
    planes = [
        [chip * PLANE_DEVICES + place for place in range(PLANE_DEVICES)]
        for chip in range(COLUMN_CHIPS)
    ]
    kv = jnp.concatenate([keys, values], axis=1)
    kv = lax.all_gather(kv, "seq", axis=0, tiled=True, axis_index_groups=columns)
    kv = lax.all_gather(kv, "seq", axis=0, tiled=True, axis_index_groups=planes)
    order = block_start.reshape(COLUMN_CHIPS, PLANE_DEVICES, 2).transpose(1, 0, 2).reshape(-1)
    count = order.shape[0]
    at = jnp.arange(count, dtype=jnp.int32)
    place = jnp.sum(
        jnp.where(order[None, :] == at[:, None] * HALF_ROWS, at[None, :], 0), axis=1
    )
    own_starts = lax.dynamic_index_in_dim(block_start, own_index, 0, keepdims=False)
    attended = attend(queries, kv, place, own_starts)
    return lax.all_to_all(attended, "tp", split_axis=0, concat_axis=1, tiled=True)


def solution(mesh):
    placed = (P("seq", "tp"), P("seq", "tp"), P("seq", "tp"), P())
    return jax.shard_map(
        on_device, mesh=mesh, in_specs=placed, out_specs=P(("seq", "tp"), None), check_vma=False
    )
```

```python
import math

import jax
import jax.numpy as jnp
from jax import lax
from jax.experimental import pallas as pl
from jax.experimental.pallas import tpu as pltpu
from jax.sharding import PartitionSpec as P

HEAD_SIZE = 128
HALF_ROWS = 64
MASKED_SCORE = -1e30
ROW_TILE = 256
CHIPS_Y, CHIPS_Z, CORES = 4, 8, 2


def seq_index(y, z, core):
    return (y * CHIPS_Z + z % CHIPS_Z) * CORES + core


PLACES = [(y, z, core) for y in range(CHIPS_Y) for z in range(CHIPS_Z) for core in range(CORES)]
COLUMNS = [
    [seq_index(y, z, core) for y in range(CHIPS_Y) for core in range(CORES)]
    for z in range(CHIPS_Z)
]
ALONG_Z = [
    (seq_index(y, z, core), seq_index(y, z + 1 - 2 * core, core)) for y, z, core in PLACES
]
OTHER_CORE = [(seq_index(*place), seq_index(*place) ^ 1) for place in PLACES]


def absorb(scaled, unit, bias_of, total, largest):
    keys = unit[:, :HEAD_SIZE]
    keys = jnp.concatenate([keys, keys], axis=1)
    ones = jnp.ones((unit.shape[0], HEAD_SIZE), jnp.bfloat16)
    values = jnp.concatenate([unit[:, HEAD_SIZE:], ones], axis=1)
    count = scaled.shape[0] // ROW_TILE

    def scores_of(tile):
        return lax.dot_general(
            scaled[tile * ROW_TILE : (tile + 1) * ROW_TILE, :],
            keys,
            (((1,), (1,)), ((), ())),
            preferred_element_type=jnp.float32,
        )

    ahead = scores_of(0)
    for tile in range(count):
        rows = slice(tile * ROW_TILE, (tile + 1) * ROW_TILE)
        scores = bias_of(ahead, tile // (count // 2))
        if tile + 1 < count:
            ahead = scores_of(tile + 1)
        old = largest[rows, :]
        new = jnp.maximum(old, jnp.max(scores, axis=1, keepdims=True))
        weights = jnp.exp2(scores - new[:, :1]).astype(jnp.bfloat16)
        fade = jnp.exp2(old - new)
        product = jnp.dot(weights, values, preferred_element_type=jnp.float32)
        total[rows, :] = total[rows, :] * jnp.concatenate([fade, fade], axis=1) + product
        largest[rows, :] = new


def first_kernel(own_ref, query_ref, unit_ref, pos_ref, scaled, total, largest):
    heads = query_ref.shape[1] // HEAD_SIZE
    scale = math.log2(math.e) / math.sqrt(HEAD_SIZE)
    for half in range(2):
        for head in range(heads):
            part = query_ref[
                half * HALF_ROWS : (half + 1) * HALF_ROWS,
                head * HEAD_SIZE : (head + 1) * HEAD_SIZE,
            ]
            part = part.astype(jnp.float32) * scale
            high = part.astype(jnp.bfloat16)
            start = (half * heads + head) * HALF_ROWS
            scaled[start : start + HALF_ROWS, :HEAD_SIZE] = high
            scaled[start : start + HALF_ROWS, HEAD_SIZE:] = (
                part - high.astype(jnp.float32)
            ).astype(jnp.bfloat16)
    total[...] = jnp.zeros_like(total)
    largest[...] = jnp.full_like(largest, MASKED_SCORE)

    def masked(scores, half):
        row_pos = own_ref[half] + lax.rem(
            lax.broadcasted_iota(jnp.int32, scores.shape, 0), HALF_ROWS
        )
        return jnp.where(pos_ref[...] <= row_pos, scores, MASKED_SCORE)

    absorb(scaled, unit_ref[...], masked, total, largest)


def next_kernel(scaled, unit_ref, bias_ref, total_in, largest_in, total, largest):
    del total_in, largest_in

    def masked(scores, half):
        return scores + bias_ref[half : half + 1, :]

    absorb(scaled, unit_ref[...], masked, total, largest)


def last_kernel(scaled, near_ref, far_ref, bias_ref, total_in, largest_in, out_ref, total, largest):
    def masked(scores, half):
        return scores + bias_ref[half : half + 1, :]

    total[...] = total_in[...]
    largest[...] = largest_in[...]
    unit = jnp.concatenate([near_ref[...], far_ref[...]], axis=0)
    absorb(scaled, unit, masked, total, largest)
    heads = out_ref.shape[1] // HEAD_SIZE
    for half in range(2):
        for head in range(heads):
            start = (half * heads + head) * HALF_ROWS
            rows = slice(start, start + HALF_ROWS)
            out_ref[
                half * HALF_ROWS : (half + 1) * HALF_ROWS,
                head * HEAD_SIZE : (head + 1) * HEAD_SIZE,
            ] = (total[rows, :HEAD_SIZE] / total[rows, HEAD_SIZE:]).astype(jnp.bfloat16)


SMEM = pl.BlockSpec(memory_space=pltpu.SMEM)
VMEM = pl.BlockSpec(memory_space=pltpu.VMEM)
PARAMS = pltpu.CompilerParams(vmem_limit_bytes=40 * 2**20)


def after_kernel(value_ref, other_ref, out_ref):
    del value_ref, other_ref, out_ref


def after(value, other):
    anywhere = pl.BlockSpec(memory_space=pl.ANY)
    return pl.pallas_call(
        after_kernel,
        out_shape=jax.ShapeDtypeStruct(value.shape, value.dtype),
        in_specs=[anywhere] * 2,
        out_specs=anywhere,
        input_output_aliases={0: 0},
        name="after",
    )(value, other)


def kernel_cost(rows, keys):
    return pl.CostEstimate(
        flops=4 * rows * keys * 2 * HEAD_SIZE,
        bytes_accessed=2 * 2**20,
        transcendentals=rows * keys,
    )


def on_device(queries, keys, values, block_start):
    own_index = lax.axis_index("seq")
    core = own_index % CORES
    own_z = (own_index // CORES) % CHIPS_Z
    row_count = queries.shape[0] * queries.shape[1] // HEAD_SIZE

    kv = jnp.concatenate([keys, values], axis=1)
    own_unit = lax.all_gather(kv, "seq", axis=0, tiled=True, axis_index_groups=COLUMNS)
    unit_rows = own_unit.shape[0]

    starts = block_start.reshape(CHIPS_Y, CHIPS_Z, CORES * 2).transpose(1, 0, 2)
    starts = starts.reshape(CHIPS_Z, -1)
    starts = jnp.concatenate([starts, starts], axis=0)
    starts = lax.dynamic_slice_in_dim(starts, own_z, CHIPS_Z, 0)
    own_starts = lax.dynamic_index_in_dim(block_start, own_index, 0, keepdims=False)
    positions = jnp.repeat(starts, HALF_ROWS, axis=1)
    own_pos = positions[:1] + lax.rem(
        lax.broadcasted_iota(jnp.int32, (1, unit_rows), 1), HALF_ROWS
    )
    bias = jnp.where(
        positions[:, None, :] < own_starts[None, :, None], 0.0, MASKED_SCORE
    ).astype(jnp.float32)

    def shape(rows, columns, dtype):
        return jax.ShapeDtypeStruct((rows, columns), dtype)

    state = [
        shape(row_count, 2 * HEAD_SIZE, jnp.float32),
        shape(row_count, HEAD_SIZE, jnp.float32),
    ]
    scaled, total, largest = pl.pallas_call(
        first_kernel,
        out_shape=[shape(row_count, 2 * HEAD_SIZE, jnp.bfloat16)] + state,
        in_specs=[SMEM] + [VMEM] * 3,
        out_specs=[VMEM] * 3,
        compiler_params=PARAMS,
        cost_estimate=kernel_cost(row_count, unit_rows),
        name="attend_first",
    )(own_starts, queries, own_unit, own_pos)

    def attend_next(unit, bias, total, largest):
        return pl.pallas_call(
            next_kernel,
            out_shape=state,
            in_specs=[VMEM] * 5,
            out_specs=[VMEM] * 2,
            input_output_aliases={3: 0, 4: 1},
            compiler_params=PARAMS,
            cost_estimate=kernel_cost(row_count, unit_rows),
            name="attend_next",
        )(scaled, unit, bias, total, largest)

    unit = lax.ppermute(own_unit, "seq", ALONG_Z)
    for step in range(1, CHIPS_Z // 2):
        unit = after(unit, largest)
        here = unit
        if step + 1 == CHIPS_Z // 2:
            unit = lax.dynamic_slice_in_dim(unit, core * (unit_rows // 2), unit_rows // 2, 0)
        unit = lax.ppermute(unit, "seq", ALONG_Z)
        other = lax.ppermute(here, "seq", OTHER_CORE)
        lower, upper = bias[CHIPS_Z - step], bias[step]
        total, largest = attend_next(
            here, jnp.where(core == 0, lower, upper), total, largest
        )
        halfway = largest
        total, largest = attend_next(
            other, jnp.where(core == 0, upper, lower), total, largest
        )
    unit = after(unit, halfway)
    other = lax.ppermute(unit, "seq", OTHER_CORE)
    opposite = bias[CHIPS_Z // 2]
    opposite = jnp.where(core == 0, opposite, jnp.roll(opposite, unit_rows // 2, axis=1))
    attended = pl.pallas_call(
        last_kernel,
        out_shape=shape(queries.shape[0], queries.shape[1], jnp.bfloat16),
        in_specs=[VMEM] * 6,
        out_specs=VMEM,
        scratch_shapes=[
            pltpu.VMEM((row_count, 2 * HEAD_SIZE), jnp.float32),
            pltpu.VMEM((row_count, HEAD_SIZE), jnp.float32),
        ],
        compiler_params=PARAMS,
        cost_estimate=kernel_cost(row_count, unit_rows),
        name="attend_last",
    )(scaled, unit, other, opposite, total, largest)
    return lax.all_to_all(attended, "tp", split_axis=0, concat_axis=1, tiled=True)


def solution(mesh):
    placed = (P("seq", "tp"), P("seq", "tp"), P("seq", "tp"), P())
    return jax.shard_map(
        on_device, mesh=mesh, in_specs=placed, out_specs=P(("seq", "tp"), None), check_vma=False
    )
```

```python
import math

import jax
import jax.numpy as jnp
from jax import lax
from jax.experimental import pallas as pl
from jax.experimental.pallas import tpu as pltpu
from jax.sharding import PartitionSpec as P

HEAD_SIZE = 128
HALF_ROWS = 64
MASKED_SCORE = -1e30
ROW_TILE = 256
CHIPS_Y, CHIPS_Z, CORES = 4, 8, 2


def seq_index(y, z, core):
    return (y * CHIPS_Z + z % CHIPS_Z) * CORES + core


PLACES = [(y, z, core) for y in range(CHIPS_Y) for z in range(CHIPS_Z) for core in range(CORES)]
COLUMNS = [
    [seq_index(y, z, core) for y in range(CHIPS_Y) for core in range(CORES)]
    for z in range(CHIPS_Z)
]
ALONG_Z = [
    (seq_index(y, z, core), seq_index(y, z + 1 - 2 * core, core)) for y, z, core in PLACES
]
OTHER_CORE = [(seq_index(*place), seq_index(*place) ^ 1) for place in PLACES]


def absorb(scaled, unit, bias_of, total, largest):
    keys = unit[:, :HEAD_SIZE]
    keys = jnp.concatenate([keys, keys], axis=1)
    ones = jnp.ones((unit.shape[0], HEAD_SIZE), jnp.bfloat16)
    values = jnp.concatenate([unit[:, HEAD_SIZE:], ones], axis=1)
    count = scaled.shape[0] // ROW_TILE

    def scores_of(tile):
        return lax.dot_general(
            scaled[tile * ROW_TILE : (tile + 1) * ROW_TILE, :],
            keys,
            (((1,), (1,)), ((), ())),
            preferred_element_type=jnp.float32,
        )

    ahead = scores_of(0)
    for tile in range(count):
        rows = slice(tile * ROW_TILE, (tile + 1) * ROW_TILE)
        scores = bias_of(ahead, tile // (count // 2))
        if tile + 1 < count:
            ahead = scores_of(tile + 1)
        old = largest[rows, :]
        new = jnp.maximum(old, jnp.max(scores, axis=1, keepdims=True))
        weights = jnp.exp2(scores - new[:, :1]).astype(jnp.bfloat16)
        fade = jnp.exp2(old - new)
        product = jnp.dot(weights, values, preferred_element_type=jnp.float32)
        total[rows, :] = total[rows, :] * jnp.concatenate([fade, fade], axis=1) + product
        largest[rows, :] = new


def first_kernel(own_ref, query_ref, unit_ref, pos_ref, scaled, total, largest):
    heads = query_ref.shape[1] // HEAD_SIZE
    scale = math.log2(math.e) / math.sqrt(HEAD_SIZE)
    for half in range(2):
        for head in range(heads):
            part = query_ref[
                half * HALF_ROWS : (half + 1) * HALF_ROWS,
                head * HEAD_SIZE : (head + 1) * HEAD_SIZE,
            ]
            part = part.astype(jnp.float32) * scale
            high = part.astype(jnp.bfloat16)
            start = (half * heads + head) * HALF_ROWS
            scaled[start : start + HALF_ROWS, :HEAD_SIZE] = high
            scaled[start : start + HALF_ROWS, HEAD_SIZE:] = (
                part - high.astype(jnp.float32)
            ).astype(jnp.bfloat16)
    total[...] = jnp.zeros_like(total)
    largest[...] = jnp.full_like(largest, MASKED_SCORE)

    def masked(scores, half):
        row_pos = own_ref[half] + lax.rem(
            lax.broadcasted_iota(jnp.int32, scores.shape, 0), HALF_ROWS
        )
        return jnp.where(pos_ref[...] <= row_pos, scores, MASKED_SCORE)

    absorb(scaled, unit_ref[...], masked, total, largest)


def next_kernel(scaled, unit_ref, bias_ref, total_in, largest_in, total, largest):
    del total_in, largest_in

    def masked(scores, half):
        return scores + bias_ref[half : half + 1, :]

    absorb(scaled, unit_ref[...], masked, total, largest)


def last_kernel(scaled, near_ref, far_ref, bias_ref, total_in, largest_in, out_ref, total, largest):
    del total_in, largest_in

    def masked(scores, half):
        return scores + bias_ref[half : half + 1, :]

    unit = jnp.concatenate([near_ref[...], far_ref[...]], axis=0)
    absorb(scaled, unit, masked, total, largest)
    heads = out_ref.shape[1] // HEAD_SIZE
    for half in range(2):
        for head in range(heads):
            start = (half * heads + head) * HALF_ROWS
            rows = slice(start, start + HALF_ROWS)
            out_ref[
                half * HALF_ROWS : (half + 1) * HALF_ROWS,
                head * HEAD_SIZE : (head + 1) * HEAD_SIZE,
            ] = (total[rows, :HEAD_SIZE] / total[rows, HEAD_SIZE:]).astype(jnp.bfloat16)


SMEM = pl.BlockSpec(memory_space=pltpu.SMEM)
VMEM = pl.BlockSpec(memory_space=pltpu.VMEM)
PARAMS = pltpu.CompilerParams(vmem_limit_bytes=16 * 2**20)


def after_kernel(*refs):
    del refs


def after(value, *others):
    anywhere = pl.BlockSpec(memory_space=pl.ANY)
    return pl.pallas_call(
        after_kernel,
        out_shape=jax.ShapeDtypeStruct(value.shape, value.dtype),
        in_specs=[anywhere] * (1 + len(others)),
        out_specs=anywhere,
        input_output_aliases={0: 0},
        compiler_params=pltpu.CompilerParams(vmem_limit_bytes=2**20),
        name="after",
    )(value, *[held(other) for other in others])


def held(value):
    return pltpu.with_memory_space_constraint(value, pltpu.VMEM)


def kernel_cost(rows, keys):
    return pl.CostEstimate(
        flops=4 * rows * keys * 2 * HEAD_SIZE,
        bytes_accessed=2 * 2**20,
        transcendentals=rows * keys,
    )


def on_device(queries, keys, values, block_start):
    own_index = lax.axis_index("seq")
    core = own_index % CORES
    own_z = (own_index // CORES) % CHIPS_Z
    row_count = queries.shape[0] * queries.shape[1] // HEAD_SIZE

    kv = jnp.concatenate([keys, values], axis=1)
    own_unit = lax.all_gather(kv, "seq", axis=0, tiled=True, axis_index_groups=COLUMNS)
    unit_rows = own_unit.shape[0]

    starts = block_start.reshape(CHIPS_Y, CHIPS_Z, CORES * 2).transpose(1, 0, 2)
    starts = starts.reshape(CHIPS_Z, -1)
    starts = jnp.concatenate([starts, starts], axis=0)
    starts = lax.dynamic_slice_in_dim(starts, own_z, CHIPS_Z, 0)
    own_starts = lax.dynamic_index_in_dim(block_start, own_index, 0, keepdims=False)
    positions = jnp.repeat(starts, HALF_ROWS, axis=1)
    own_pos = positions[:1] + lax.rem(
        lax.broadcasted_iota(jnp.int32, (1, unit_rows), 1), HALF_ROWS
    )
    bias = jnp.where(
        positions[:, None, :] < own_starts[None, :, None], 0.0, MASKED_SCORE
    ).astype(jnp.float32)

    def shape(rows, columns, dtype):
        return jax.ShapeDtypeStruct((rows, columns), dtype)

    state = [
        pltpu.VMEM((row_count, 2 * HEAD_SIZE), jnp.float32),
        pltpu.VMEM((row_count, HEAD_SIZE), jnp.float32),
    ]
    scaled, total, largest = pl.pallas_call(
        first_kernel,
        out_shape=[pltpu.VMEM((row_count, 2 * HEAD_SIZE), jnp.bfloat16)] + state,
        in_specs=[SMEM] + [VMEM] * 3,
        out_specs=[VMEM] * 3,
        compiler_params=PARAMS,
        cost_estimate=kernel_cost(row_count, unit_rows),
        name="attend_first",
    )(own_starts, queries, own_unit, own_pos)

    def attend_next(unit, bias, total, largest):
        return pl.pallas_call(
            next_kernel,
            out_shape=state,
            in_specs=[VMEM] * 5,
            out_specs=[VMEM] * 2,
            input_output_aliases={3: 0, 4: 1},
            compiler_params=PARAMS,
            cost_estimate=kernel_cost(row_count, unit_rows),
            name="attend_next",
        )(held(scaled), unit, bias, held(total), held(largest))

    unit = lax.ppermute(own_unit, "seq", ALONG_Z)
    for step in range(1, CHIPS_Z // 2):
        unit = after(unit, largest)
        here = unit
        if step + 1 == CHIPS_Z // 2:
            unit = lax.dynamic_slice_in_dim(unit, core * (unit_rows // 2), unit_rows // 2, 0)
        unit = lax.ppermute(unit, "seq", ALONG_Z)
        other = lax.ppermute(here, "seq", OTHER_CORE)
        lower, upper = bias[CHIPS_Z - step], bias[step]
        total, largest = attend_next(
            here, jnp.where(core == 0, lower, upper), total, largest
        )
        total, largest = attend_next(
            other, jnp.where(core == 0, upper, lower), total, largest
        )
    unit = after(unit, largest)
    other = lax.ppermute(unit, "seq", OTHER_CORE)
    opposite = bias[CHIPS_Z // 2]
    opposite = jnp.where(core == 0, opposite, jnp.roll(opposite, unit_rows // 2, axis=1))
    attended, _, _ = pl.pallas_call(
        last_kernel,
        out_shape=[shape(queries.shape[0], queries.shape[1], jnp.bfloat16)] + state,
        in_specs=[VMEM] * 6,
        out_specs=[VMEM] * 3,
        input_output_aliases={4: 1, 5: 2},
        compiler_params=PARAMS,
        cost_estimate=kernel_cost(row_count, unit_rows),
        name="attend_last",
    )(held(scaled), unit, other, opposite, held(total), held(largest))
    return lax.all_to_all(attended, "tp", split_axis=0, concat_axis=1, tiled=True)


def solution(mesh):
    placed = (P("seq", "tp"), P("seq", "tp"), P("seq", "tp"), P())
    return jax.shard_map(
        on_device, mesh=mesh, in_specs=placed, out_specs=P(("seq", "tp"), None), check_vma=False
    )
```

```python
import functools
import math

import jax
import jax.numpy as jnp
from jax import lax
from jax.experimental import pallas as pl
from jax.experimental.pallas import tpu as pltpu
from jax.sharding import PartitionSpec as P

HEAD_SIZE = 128
HALF_ROWS = 64
MASKED_SCORE = -1e30
ROW_TILE = 256
CHIPS_Y, CHIPS_Z, CORES = 4, 8, 2


def seq_index(y, z, core):
    return (y * CHIPS_Z + z % CHIPS_Z) * CORES + core


PLACES = [(y, z, core) for y in range(CHIPS_Y) for z in range(CHIPS_Z) for core in range(CORES)]
COLUMNS = [
    [seq_index(y, z, core) for y in range(CHIPS_Y) for core in range(CORES)]
    for z in range(CHIPS_Z)
]
ALONG_Z = [
    (seq_index(y, z, core), seq_index(y, z + 1 - 2 * core, core)) for y, z, core in PLACES
]
OTHER_CORE = [(seq_index(*place), seq_index(*place) ^ 1) for place in PLACES]


def absorb(scaled, unit, bias_of, total, largest):
    keys = unit[:, :HEAD_SIZE]
    keys = jnp.concatenate([keys, keys], axis=1)
    ones = jnp.ones((unit.shape[0], HEAD_SIZE), jnp.bfloat16)
    values = jnp.concatenate([unit[:, HEAD_SIZE:], ones], axis=1)
    count = scaled.shape[0] // ROW_TILE

    def scores_of(tile):
        return lax.dot_general(
            scaled[tile * ROW_TILE : (tile + 1) * ROW_TILE, :],
            keys,
            (((1,), (1,)), ((), ())),
            preferred_element_type=jnp.float32,
        )

    ahead = scores_of(0)
    for tile in range(count):
        rows = slice(tile * ROW_TILE, (tile + 1) * ROW_TILE)
        scores = bias_of(ahead, tile // (count // 2))
        if tile + 1 < count:
            ahead = scores_of(tile + 1)
        old = largest[rows, :]
        new = jnp.maximum(old, jnp.max(scores, axis=1, keepdims=True))
        weights = jnp.exp2(scores - new[:, :1]).astype(jnp.bfloat16)
        fade = jnp.exp2(old - new)
        product = jnp.dot(weights, values, preferred_element_type=jnp.float32)
        total[rows, :] = total[rows, :] * jnp.concatenate([fade, fade], axis=1) + product
        largest[rows, :] = new


def first_kernel(own_ref, query_ref, unit_ref, pos_ref, bias_ref, scaled, total, largest):
    del bias_ref
    heads = query_ref.shape[1] // HEAD_SIZE
    scale = math.log2(math.e) / math.sqrt(HEAD_SIZE)
    for half in range(2):
        for head in range(heads):
            part = query_ref[
                half * HALF_ROWS : (half + 1) * HALF_ROWS,
                head * HEAD_SIZE : (head + 1) * HEAD_SIZE,
            ]
            part = part.astype(jnp.float32) * scale
            high = part.astype(jnp.bfloat16)
            start = (half * heads + head) * HALF_ROWS
            scaled[start : start + HALF_ROWS, :HEAD_SIZE] = high
            scaled[start : start + HALF_ROWS, HEAD_SIZE:] = (
                part - high.astype(jnp.float32)
            ).astype(jnp.bfloat16)
    total[...] = jnp.zeros_like(total)
    largest[...] = jnp.full_like(largest, MASKED_SCORE)

    def masked(scores, half):
        row_pos = own_ref[half] + lax.rem(
            lax.broadcasted_iota(jnp.int32, scores.shape, 0), HALF_ROWS
        )
        return jnp.where(pos_ref[...] <= row_pos, scores, MASKED_SCORE)

    absorb(scaled, unit_ref[...], masked, total, largest)


def next_kernel(turn, scaled, unit_ref, bias_ref, total_in, largest_in, total, largest):
    del total_in, largest_in

    def masked(scores, half):
        row = 2 * turn + half
        return scores + bias_ref[row : row + 1, :]

    absorb(scaled, unit_ref[...], masked, total, largest)


def last_kernel(turn, scaled, unit_ref, bias_ref, total_in, largest_in, out_ref, total, largest):
    del total_in, largest_in

    def masked(scores, half):
        row = 2 * turn + half
        return scores + bias_ref[row : row + 1, :]

    absorb(scaled, unit_ref[...], masked, total, largest)
    heads = out_ref.shape[1] // HEAD_SIZE
    for half in range(2):
        for head in range(heads):
            start = (half * heads + head) * HALF_ROWS
            rows = slice(start, start + HALF_ROWS)
            out_ref[
                half * HALF_ROWS : (half + 1) * HALF_ROWS,
                head * HEAD_SIZE : (head + 1) * HEAD_SIZE,
            ] = (total[rows, :HEAD_SIZE] / total[rows, HEAD_SIZE:]).astype(jnp.bfloat16)


SMEM = pl.BlockSpec(memory_space=pltpu.SMEM)
VMEM = pl.BlockSpec(memory_space=pltpu.VMEM)
PARAMS = pltpu.CompilerParams(vmem_limit_bytes=16 * 2**20)


def after_kernel(*refs):
    del refs


def after(value, *others):
    anywhere = pl.BlockSpec(memory_space=pl.ANY)
    return pl.pallas_call(
        after_kernel,
        out_shape=jax.ShapeDtypeStruct(value.shape, value.dtype),
        in_specs=[anywhere] * (1 + len(others)),
        out_specs=anywhere,
        input_output_aliases={0: 0},
        compiler_params=pltpu.CompilerParams(vmem_limit_bytes=2**20),
        name="after",
    )(value, *[held(other) for other in others])


def held(value):
    return pltpu.with_memory_space_constraint(value, pltpu.VMEM)


def kernel_cost(rows, keys):
    return pl.CostEstimate(
        flops=4 * rows * keys * 2 * HEAD_SIZE,
        bytes_accessed=2 * 2**20,
        transcendentals=rows * keys,
    )


def on_device(queries, keys, values, block_start):
    own_index = lax.axis_index("seq")
    core = own_index % CORES
    own_z = (own_index // CORES) % CHIPS_Z
    row_count = queries.shape[0] * queries.shape[1] // HEAD_SIZE

    kv = jnp.concatenate([keys, values], axis=1)
    own_unit = lax.all_gather(kv, "seq", axis=0, tiled=True, axis_index_groups=COLUMNS)
    unit_rows = own_unit.shape[0]

    starts = block_start.reshape(CHIPS_Y, CHIPS_Z, CORES * 2).transpose(1, 0, 2)
    starts = starts.reshape(CHIPS_Z, -1)
    starts = jnp.concatenate([starts, starts], axis=0)
    starts = lax.dynamic_slice_in_dim(starts, own_z, CHIPS_Z, 0)
    own_starts = lax.dynamic_index_in_dim(block_start, own_index, 0, keepdims=False)
    positions = jnp.repeat(starts, HALF_ROWS, axis=1)
    own_pos = positions[:1] + lax.rem(
        lax.broadcasted_iota(jnp.int32, (1, unit_rows), 1), HALF_ROWS
    )
    distances = [
        distance
        for step in range(1, CHIPS_Z // 2)
        for distance in (CHIPS_Z - step, step)
    ] + [CHIPS_Z // 2]
    forward = jnp.stack([positions[distance] for distance in distances])
    backward = jnp.stack([positions[CHIPS_Z - distance] for distance in distances])
    bias = jnp.where(
        jnp.where(core == 0, forward, backward)[:, None, :] < own_starts[None, :, None],
        0.0,
        MASKED_SCORE,
    ).astype(jnp.float32)
    bias = bias.reshape(-1, unit_rows)

    def shape(rows, columns, dtype):
        return jax.ShapeDtypeStruct((rows, columns), dtype)

    state = [
        pltpu.VMEM((row_count, 2 * HEAD_SIZE), jnp.float32),
        pltpu.VMEM((row_count, HEAD_SIZE), jnp.float32),
    ]
    scaled, total, largest = pl.pallas_call(
        first_kernel,
        out_shape=[pltpu.VMEM((row_count, 2 * HEAD_SIZE), jnp.bfloat16)] + state,
        in_specs=[SMEM] + [VMEM] * 3 + [pl.BlockSpec(memory_space=pl.ANY)],
        out_specs=[VMEM] * 3,
        compiler_params=PARAMS,
        cost_estimate=kernel_cost(row_count, unit_rows),
        name="attend_first",
    )(own_starts, queries, own_unit, own_pos, bias)

    def attend_next(turn, unit, total, largest):
        return pl.pallas_call(
            functools.partial(next_kernel, turn),
            out_shape=state,
            in_specs=[VMEM] * 5,
            out_specs=[VMEM] * 2,
            input_output_aliases={3: 0, 4: 1},
            compiler_params=PARAMS,
            cost_estimate=kernel_cost(row_count, unit_rows),
            name="attend_next",
        )(held(scaled), unit, bias, held(total), held(largest))

    unit = lax.ppermute(own_unit, "seq", ALONG_Z)
    here = after(unit, largest)
    unit = lax.ppermute(here, "seq", ALONG_Z)
    total, largest = attend_next(0, here, total, largest)
    other = lax.ppermute(after(here, largest), "seq", OTHER_CORE)
    for step in range(2, CHIPS_Z // 2):
        here = after(unit, largest)
        unit = lax.ppermute(here, "seq", ALONG_Z)
        total, largest = attend_next(2 * step - 3, other, total, largest)
        other = lax.ppermute(after(here, largest), "seq", OTHER_CORE)
        total, largest = attend_next(2 * step - 2, here, total, largest)
    unit = after(unit, largest)
    total, largest = attend_next(len(distances) - 2, other, total, largest)
    attended, _, _ = pl.pallas_call(
        functools.partial(last_kernel, len(distances) - 1),
        out_shape=[shape(queries.shape[0], queries.shape[1], jnp.bfloat16)] + state,
        in_specs=[VMEM] * 5,
        out_specs=[VMEM] * 3,
        input_output_aliases={3: 1, 4: 2},
        compiler_params=PARAMS,
        cost_estimate=kernel_cost(row_count, unit_rows),
        name="attend_last",
    )(held(scaled), unit, bias, held(total), held(largest))
    return lax.all_to_all(attended, "tp", split_axis=0, concat_axis=1, tiled=True)


def solution(mesh):
    placed = (P("seq", "tp"), P("seq", "tp"), P("seq", "tp"), P())
    return jax.shard_map(
        on_device, mesh=mesh, in_specs=placed, out_specs=P(("seq", "tp"), None), check_vma=False
    )
```

```python
import functools
import math

import jax
import jax.numpy as jnp
from jax import lax
from jax.experimental import pallas as pl
from jax.experimental.pallas import tpu as pltpu
from jax.sharding import PartitionSpec as P

HEAD_SIZE = 128
HALF_ROWS = 64
MASKED_SCORE = -1e30
ROW_TILE = 512
CHIPS_Y, CHIPS_Z, CORES = 4, 8, 2


def seq_index(y, z, core):
    return (y * CHIPS_Z + z % CHIPS_Z) * CORES + core


PLACES = [(y, z, core) for y in range(CHIPS_Y) for z in range(CHIPS_Z) for core in range(CORES)]
COLUMNS = [
    [seq_index(y, z, core) for y in range(CHIPS_Y) for core in range(CORES)]
    for z in range(CHIPS_Z)
]
ALONG_Z = [
    (seq_index(y, z, core), seq_index(y, z + 1 - 2 * core, core)) for y, z, core in PLACES
]
OTHER_CORE = [(seq_index(*place), seq_index(*place) ^ 1) for place in PLACES]


def absorb(scaled, unit, bias_of, total, largest):
    keys = unit[:, :HEAD_SIZE]
    keys = jnp.concatenate([keys, keys], axis=1)
    ones = jnp.ones((unit.shape[0], HEAD_SIZE), jnp.bfloat16)
    values = jnp.concatenate([unit[:, HEAD_SIZE:], ones], axis=1)
    count = scaled.shape[0] // ROW_TILE

    def scores_of(tile):
        return lax.dot_general(
            scaled[tile * ROW_TILE : (tile + 1) * ROW_TILE, :],
            keys,
            (((1,), (1,)), ((), ())),
            preferred_element_type=jnp.float32,
        )

    ahead = scores_of(0)
    for tile in range(count):
        rows = slice(tile * ROW_TILE, (tile + 1) * ROW_TILE)
        scores = bias_of(ahead, tile // (count // 2))
        if tile + 1 < count:
            ahead = scores_of(tile + 1)
        old = largest[rows, :]
        new = jnp.maximum(old, jnp.max(scores, axis=1, keepdims=True))
        level = jnp.concatenate([new] * (unit.shape[0] // HEAD_SIZE), axis=1)
        weights = jnp.exp2(scores - level).astype(jnp.bfloat16)
        fade = jnp.exp2(old - new)
        product = jnp.dot(weights, values, preferred_element_type=jnp.float32)
        total[rows, :] = total[rows, :] * jnp.concatenate([fade, fade], axis=1) + product
        largest[rows, :] = new


def first_kernel(own_ref, query_ref, unit_ref, pos_ref, bias_ref, scaled, total, largest):
    del bias_ref
    heads = query_ref.shape[1] // HEAD_SIZE
    scale = math.log2(math.e) / math.sqrt(HEAD_SIZE)
    for half in range(2):
        for head in range(heads):
            part = query_ref[
                half * HALF_ROWS : (half + 1) * HALF_ROWS,
                head * HEAD_SIZE : (head + 1) * HEAD_SIZE,
            ]
            part = part.astype(jnp.float32) * scale
            high = part.astype(jnp.bfloat16)
            start = (half * heads + head) * HALF_ROWS
            scaled[start : start + HALF_ROWS, :HEAD_SIZE] = high
            scaled[start : start + HALF_ROWS, HEAD_SIZE:] = (
                part - high.astype(jnp.float32)
            ).astype(jnp.bfloat16)
    total[...] = jnp.zeros_like(total)
    largest[...] = jnp.full_like(largest, MASKED_SCORE)

    def masked(scores, half):
        row_pos = own_ref[half] + lax.rem(
            lax.broadcasted_iota(jnp.int32, scores.shape, 0), HALF_ROWS
        )
        return jnp.where(pos_ref[...] <= row_pos, scores, MASKED_SCORE)

    absorb(scaled, unit_ref[...], masked, total, largest)


def next_kernel(turn, scaled, unit_ref, bias_ref, total_in, largest_in, total, largest):
    del total_in, largest_in

    def masked(scores, half):
        row = 2 * turn + half
        return scores + bias_ref[row : row + 1, :]

    absorb(scaled, unit_ref[...], masked, total, largest)


def last_kernel(turn, scaled, unit_ref, bias_ref, total_in, largest_in, out_ref, total, largest):
    del total_in, largest_in

    def masked(scores, half):
        row = 2 * turn + half
        return scores + bias_ref[row : row + 1, :]

    absorb(scaled, unit_ref[...], masked, total, largest)
    heads = out_ref.shape[1] // HEAD_SIZE
    for half in range(2):
        for head in range(heads):
            start = (half * heads + head) * HALF_ROWS
            rows = slice(start, start + HALF_ROWS)
            out_ref[
                half * HALF_ROWS : (half + 1) * HALF_ROWS,
                head * HEAD_SIZE : (head + 1) * HEAD_SIZE,
            ] = (total[rows, :HEAD_SIZE] / total[rows, HEAD_SIZE:]).astype(jnp.bfloat16)


SMEM = pl.BlockSpec(memory_space=pltpu.SMEM)
VMEM = pl.BlockSpec(memory_space=pltpu.VMEM)
PARAMS = pltpu.CompilerParams(vmem_limit_bytes=16 * 2**20)


def after_kernel(*refs):
    del refs


def after(value, *others):
    anywhere = pl.BlockSpec(memory_space=pl.ANY)
    return pl.pallas_call(
        after_kernel,
        out_shape=jax.ShapeDtypeStruct(value.shape, value.dtype),
        in_specs=[anywhere] * (1 + len(others)),
        out_specs=anywhere,
        input_output_aliases={0: 0},
        compiler_params=pltpu.CompilerParams(vmem_limit_bytes=2**20),
        name="after",
    )(value, *[held(other) for other in others])


def held(value):
    return pltpu.with_memory_space_constraint(value, pltpu.VMEM)


def kernel_cost(rows, keys):
    return pl.CostEstimate(
        flops=4 * rows * keys * 2 * HEAD_SIZE,
        bytes_accessed=2 * 2**20,
        transcendentals=rows * keys,
    )


def on_device(queries, keys, values, block_start):
    own_index = lax.axis_index("seq")
    core = own_index % CORES
    own_z = (own_index // CORES) % CHIPS_Z
    row_count = queries.shape[0] * queries.shape[1] // HEAD_SIZE

    kv = jnp.concatenate([keys, values], axis=1)
    own_unit = lax.all_gather(kv, "seq", axis=0, tiled=True, axis_index_groups=COLUMNS)
    unit_rows = own_unit.shape[0]

    starts = block_start.reshape(CHIPS_Y, CHIPS_Z, CORES * 2).transpose(1, 0, 2)
    starts = starts.reshape(CHIPS_Z, -1)
    starts = jnp.concatenate([starts, starts], axis=0)
    starts = lax.dynamic_slice_in_dim(starts, own_z, CHIPS_Z, 0)
    own_starts = lax.dynamic_index_in_dim(block_start, own_index, 0, keepdims=False)
    positions = jnp.repeat(starts, HALF_ROWS, axis=1)
    own_pos = positions[:1] + lax.rem(
        lax.broadcasted_iota(jnp.int32, (1, unit_rows), 1), HALF_ROWS
    )
    distances = [
        distance
        for step in range(1, CHIPS_Z // 2)
        for distance in (CHIPS_Z - step, step)
    ] + [CHIPS_Z // 2]
    forward = jnp.stack([positions[distance] for distance in distances])
    backward = jnp.stack([positions[CHIPS_Z - distance] for distance in distances])
    bias = jnp.where(
        jnp.where(core == 0, forward, backward)[:, None, :] < own_starts[None, :, None],
        0.0,
        MASKED_SCORE,
    ).astype(jnp.float32)
    bias = bias.reshape(-1, unit_rows)

    def shape(rows, columns, dtype):
        return jax.ShapeDtypeStruct((rows, columns), dtype)

    state = [
        pltpu.VMEM((row_count, 2 * HEAD_SIZE), jnp.float32),
        pltpu.VMEM((row_count, HEAD_SIZE), jnp.float32),
    ]
    scaled, total, largest = pl.pallas_call(
        first_kernel,
        out_shape=[pltpu.VMEM((row_count, 2 * HEAD_SIZE), jnp.bfloat16)] + state,
        in_specs=[SMEM] + [VMEM] * 3 + [pl.BlockSpec(memory_space=pl.ANY)],
        out_specs=[VMEM] * 3,
        compiler_params=PARAMS,
        cost_estimate=kernel_cost(row_count, unit_rows),
        name="attend_first",
    )(own_starts, queries, own_unit, own_pos, bias)

    def attend_next(turn, unit, total, largest):
        return pl.pallas_call(
            functools.partial(next_kernel, turn),
            out_shape=state,
            in_specs=[VMEM] * 5,
            out_specs=[VMEM] * 2,
            input_output_aliases={3: 0, 4: 1},
            compiler_params=PARAMS,
            cost_estimate=kernel_cost(row_count, unit_rows),
            name="attend_next",
        )(held(scaled), unit, bias, held(total), held(largest))

    unit = lax.ppermute(own_unit, "seq", ALONG_Z)
    here = after(unit, largest)
    unit = lax.ppermute(here, "seq", ALONG_Z)
    total, largest = attend_next(0, here, total, largest)
    other = lax.ppermute(after(here, largest), "seq", OTHER_CORE)
    for step in range(2, CHIPS_Z // 2):
        here = after(unit, largest)
        unit = lax.ppermute(here, "seq", ALONG_Z)
        total, largest = attend_next(2 * step - 3, other, total, largest)
        other = lax.ppermute(after(here, largest), "seq", OTHER_CORE)
        total, largest = attend_next(2 * step - 2, here, total, largest)
    unit = after(unit, largest)
    total, largest = attend_next(len(distances) - 2, other, total, largest)
    attended, _, _ = pl.pallas_call(
        functools.partial(last_kernel, len(distances) - 1),
        out_shape=[shape(queries.shape[0], queries.shape[1], jnp.bfloat16)] + state,
        in_specs=[VMEM] * 5,
        out_specs=[VMEM] * 3,
        input_output_aliases={3: 1, 4: 2},
        compiler_params=PARAMS,
        cost_estimate=kernel_cost(row_count, unit_rows),
        name="attend_last",
    )(held(scaled), unit, bias, held(total), held(largest))
    return lax.all_to_all(attended, "tp", split_axis=0, concat_axis=1, tiled=True)


def solution(mesh):
    placed = (P("seq", "tp"), P("seq", "tp"), P("seq", "tp"), P())
    return jax.shard_map(
        on_device, mesh=mesh, in_specs=placed, out_specs=P(("seq", "tp"), None), check_vma=False
    )
```

```python
import functools
import math

import jax
import jax.numpy as jnp
from jax import lax
from jax.experimental import pallas as pl
from jax.experimental.pallas import tpu as pltpu
from jax.sharding import PartitionSpec as P

HEAD_SIZE = 128
HALF_ROWS = 64
MASKED_SCORE = -1e30
ROW_TILE = 256
CHIPS_Y, CHIPS_Z, CORES = 4, 8, 2


def seq_index(y, z, core):
    return (y * CHIPS_Z + z % CHIPS_Z) * CORES + core


PLACES = [(y, z, core) for y in range(CHIPS_Y) for z in range(CHIPS_Z) for core in range(CORES)]
COLUMNS = [
    [seq_index(y, z, core) for y in range(CHIPS_Y) for core in range(CORES)]
    for z in range(CHIPS_Z)
]
ALONG_Z = [
    (seq_index(y, z, core), seq_index(y, z + 1 - 2 * core, core)) for y, z, core in PLACES
]
OTHER_CORE = [(seq_index(*place), seq_index(*place) ^ 1) for place in PLACES]


def absorb(scaled, unit, bias_of, total, largest):
    keys = unit[:, :HEAD_SIZE]
    keys = jnp.concatenate([keys, keys], axis=1)
    ones = jnp.ones((unit.shape[0], HEAD_SIZE), jnp.bfloat16)
    values = jnp.concatenate([unit[:, HEAD_SIZE:], ones], axis=1)
    count = scaled.shape[0] // ROW_TILE

    def scores_of(tile):
        return lax.dot_general(
            scaled[tile * ROW_TILE : (tile + 1) * ROW_TILE, :],
            keys,
            (((1,), (1,)), ((), ())),
            preferred_element_type=jnp.float32,
        )

    ahead = scores_of(0)
    for tile in range(count):
        rows = slice(tile * ROW_TILE, (tile + 1) * ROW_TILE)
        scores = bias_of(ahead, tile // (count // 2))
        if tile + 1 < count:
            ahead = scores_of(tile + 1)
        old = largest[rows, :]
        new = jnp.maximum(old, jnp.max(scores, axis=1, keepdims=True))
        level = jnp.concatenate([new] * (unit.shape[0] // HEAD_SIZE), axis=1)
        weights = jnp.exp2(scores - level).astype(jnp.bfloat16)
        fade = jnp.exp2(old - new)
        product = jnp.dot(weights, values, preferred_element_type=jnp.float32)
        total[rows, :] = total[rows, :] * jnp.concatenate([fade, fade], axis=1) + product
        largest[rows, :] = new


def first_kernel(own_ref, query_ref, unit_ref, pos_ref, bias_ref, scaled, total, largest):
    del bias_ref
    heads = query_ref.shape[1] // HEAD_SIZE
    scale = math.log2(math.e) / math.sqrt(HEAD_SIZE)
    for half in range(2):
        for head in range(heads):
            part = query_ref[
                half * HALF_ROWS : (half + 1) * HALF_ROWS,
                head * HEAD_SIZE : (head + 1) * HEAD_SIZE,
            ]
            part = part.astype(jnp.float32) * scale
            high = part.astype(jnp.bfloat16)
            start = (half * heads + head) * HALF_ROWS
            scaled[start : start + HALF_ROWS, :HEAD_SIZE] = high
            scaled[start : start + HALF_ROWS, HEAD_SIZE:] = (
                part - high.astype(jnp.float32)
            ).astype(jnp.bfloat16)
    total[...] = jnp.zeros_like(total)
    largest[...] = jnp.full_like(largest, MASKED_SCORE)

    def masked(scores, half):
        row_pos = own_ref[half] + lax.rem(
            lax.broadcasted_iota(jnp.int32, scores.shape, 0), HALF_ROWS
        )
        return jnp.where(pos_ref[...] <= row_pos, scores, MASKED_SCORE)

    absorb(scaled, unit_ref[...], masked, total, largest)


def next_kernel(turn, scaled, unit_ref, bias_ref, total_in, largest_in, total, largest):
    del total_in, largest_in

    def masked(scores, half):
        row = 2 * turn + half
        return scores + bias_ref[row : row + 1, :]

    absorb(scaled, unit_ref[...], masked, total, largest)


def last_kernel(turn, scaled, unit_ref, bias_ref, total_in, largest_in, out_ref, total, largest):
    del total_in, largest_in

    def masked(scores, half):
        row = 2 * turn + half
        return scores + bias_ref[row : row + 1, :]

    absorb(scaled, unit_ref[...], masked, total, largest)
    heads = out_ref.shape[1] // HEAD_SIZE
    for half in range(2):
        for head in range(heads):
            start = (half * heads + head) * HALF_ROWS
            rows = slice(start, start + HALF_ROWS)
            out_ref[
                half * HALF_ROWS : (half + 1) * HALF_ROWS,
                head * HEAD_SIZE : (head + 1) * HEAD_SIZE,
            ] = (total[rows, :HEAD_SIZE] / total[rows, HEAD_SIZE:]).astype(jnp.bfloat16)


SMEM = pl.BlockSpec(memory_space=pltpu.SMEM)
VMEM = pl.BlockSpec(memory_space=pltpu.VMEM)
PARAMS = pltpu.CompilerParams(vmem_limit_bytes=16 * 2**20)


def after_kernel(*refs):
    del refs


def after(value, *others):
    anywhere = pl.BlockSpec(memory_space=pl.ANY)
    return pl.pallas_call(
        after_kernel,
        out_shape=jax.ShapeDtypeStruct(value.shape, value.dtype),
        in_specs=[anywhere] * (1 + len(others)),
        out_specs=anywhere,
        input_output_aliases={0: 0},
        compiler_params=pltpu.CompilerParams(vmem_limit_bytes=2**20),
        name="after",
    )(value, *[held(other) for other in others])


def held(value):
    return pltpu.with_memory_space_constraint(value, pltpu.VMEM)


def kernel_cost(rows, keys):
    return pl.CostEstimate(
        flops=4 * rows * keys * 2 * HEAD_SIZE,
        bytes_accessed=2 * 2**20,
        transcendentals=rows * keys,
    )


def on_device(queries, keys, values, block_start):
    own_index = lax.axis_index("seq")
    core = own_index % CORES
    own_z = (own_index // CORES) % CHIPS_Z
    row_count = queries.shape[0] * queries.shape[1] // HEAD_SIZE

    kv = jnp.concatenate([keys, values], axis=1)
    own_unit = lax.all_gather(kv, "seq", axis=0, tiled=True, axis_index_groups=COLUMNS)
    unit_rows = own_unit.shape[0]

    starts = block_start.reshape(CHIPS_Y, CHIPS_Z, CORES * 2).transpose(1, 0, 2)
    starts = starts.reshape(CHIPS_Z, -1)
    starts = jnp.concatenate([starts, starts], axis=0)
    starts = lax.dynamic_slice_in_dim(starts, own_z, CHIPS_Z, 0)
    own_starts = lax.dynamic_index_in_dim(block_start, own_index, 0, keepdims=False)
    positions = jnp.repeat(starts, HALF_ROWS, axis=1)
    own_pos = positions[:1] + lax.rem(
        lax.broadcasted_iota(jnp.int32, (1, unit_rows), 1), HALF_ROWS
    )
    distances = [
        distance
        for step in range(1, CHIPS_Z // 2)
        for distance in (CHIPS_Z - step, step)
    ] + [CHIPS_Z // 2]
    forward = jnp.stack([positions[distance] for distance in distances])
    backward = jnp.stack([positions[CHIPS_Z - distance] for distance in distances])
    bias = jnp.where(
        jnp.where(core == 0, forward, backward)[:, None, :] < own_starts[None, :, None],
        0.0,
        MASKED_SCORE,
    ).astype(jnp.float32)
    bias = bias.reshape(-1, unit_rows)

    def shape(rows, columns, dtype):
        return jax.ShapeDtypeStruct((rows, columns), dtype)

    state = [
        pltpu.VMEM((row_count, 2 * HEAD_SIZE), jnp.float32),
        pltpu.VMEM((row_count, HEAD_SIZE), jnp.float32),
    ]
    scaled, total, largest = pl.pallas_call(
        first_kernel,
        out_shape=[pltpu.VMEM((row_count, 2 * HEAD_SIZE), jnp.bfloat16)] + state,
        in_specs=[SMEM] + [VMEM] * 3 + [pl.BlockSpec(memory_space=pl.ANY)],
        out_specs=[VMEM] * 3,
        compiler_params=PARAMS,
        cost_estimate=kernel_cost(row_count, unit_rows),
        name="attend_first",
    )(own_starts, queries, own_unit, own_pos, bias)

    def attend_next(turn, unit, total, largest):
        return pl.pallas_call(
            functools.partial(next_kernel, turn),
            out_shape=state,
            in_specs=[VMEM] * 5,
            out_specs=[VMEM] * 2,
            input_output_aliases={3: 0, 4: 1},
            compiler_params=PARAMS,
            cost_estimate=kernel_cost(row_count, unit_rows),
            name="attend_next",
        )(held(scaled), unit, bias, held(total), held(largest))

    unit = lax.ppermute(own_unit, "seq", ALONG_Z)
    here = after(unit, largest)
    unit = lax.ppermute(here, "seq", ALONG_Z)
    total, largest = attend_next(0, here, total, largest)
    other = lax.ppermute(after(here, largest), "seq", OTHER_CORE)
    for step in range(2, CHIPS_Z // 2):
        here = after(unit, largest)
        unit = lax.ppermute(here, "seq", ALONG_Z)
        total, largest = attend_next(2 * step - 3, other, total, largest)
        other = lax.ppermute(after(here, largest), "seq", OTHER_CORE)
        total, largest = attend_next(2 * step - 2, here, total, largest)
    unit = after(unit, largest)
    total, largest = attend_next(len(distances) - 2, other, total, largest)
    attended, _, _ = pl.pallas_call(
        functools.partial(last_kernel, len(distances) - 1),
        out_shape=[shape(queries.shape[0], queries.shape[1], jnp.bfloat16)] + state,
        in_specs=[VMEM] * 5,
        out_specs=[VMEM] * 3,
        input_output_aliases={3: 1, 4: 2},
        compiler_params=PARAMS,
        cost_estimate=kernel_cost(row_count, unit_rows),
        name="attend_last",
    )(held(scaled), unit, bias, held(total), held(largest))
    return lax.all_to_all(attended, "tp", split_axis=0, concat_axis=1, tiled=True)


def solution(mesh):
    placed = (P("seq", "tp"), P("seq", "tp"), P("seq", "tp"), P())
    return jax.shard_map(
        on_device, mesh=mesh, in_specs=placed, out_specs=P(("seq", "tp"), None), check_vma=False
    )
```
